32 devices in a mesh: groups: 2 (over y), gx: 8 (over z, x), yz: 2 (over core).
Axes of the slice: x: 2, y: 2, z: 4, core: 2. Of those that a mesh axis runs over, the one named last changes fastest.
Arguments:
- tokens: bfloat16 [64, 18432], P(('groups', 'gx'), 'yz'), parts along dimension 0, may hold values from -80 to 80
- w_query: bfloat16 [18432, 6144], P('yz', 'gx'), may hold values from -0.046875 to 0.046875
- w_keyval: bfloat16 [18432, 512], P('yz', 'gx'), may hold values from -0.046875 to 0.046875
- w_inner: bfloat16 [18432, 9216], P('yz', 'gx'), may hold values from -0.046875 to 0.046875
- w_outer: bfloat16 [9216, 18432], P('gx', 'yz'), may hold values from -0.0625 to 0.0625
- w_attn_out: bfloat16 [6144, 18432], P('gx', 'yz'), may hold values from -0.4375 to 0.4375
- key_cache: bfloat16 [64, 2048, 256], P(('groups', 'gx', 'yz')), parts along dimension 0, may hold values from -1300 to 1300
- value_cache: bfloat16 [64, 2048, 256], P(('groups', 'gx', 'yz')), parts along dimension 0, may hold values from -6 to 6
- lengths: int32 [64], P(('groups', 'gx', 'yz')), parts along dimension 0, may hold values from 2 to 2048, as said below
Outputs:
- mixed: bfloat16 [64, 18432], P(('groups', 'gx'), 'yz'), parts along dimension 0
The draws below stay inside these ranges and needn't reach their ends.
There are 2 independent parts, one for each index of `groups`. The reference program is written for one: setup_inputs(seed, part) draws one part's arguments, and reference() takes and returns one part's arrays. A program takes and returns all parts, laid end to end along the dimension named above; an argument that names none is the same for every part. Nothing has to cross between parts.
Inputs may be any that keep to these rules, and one draw needn't show every extreme that they name: `lengths`: each request has at least two cached positions; some request in every draw has all 2048.
All inputs are finite; a program needn't handle non-finite values.
Results may differ from the reference program's by a relative error of at most 0.006.
The reference program's roundings to bfloat16 on the way count: a program that leaves them out, or rounds other values in their place, can miss the bound.
Values may be sent and summed in bfloat16 or wider, within the bound.
A program may use at most 192 MiB of HBM per device.

```python
import jax
import jax.numpy as jnp
from jax import lax

D = 18432
HEADS = 24
HEAD = 256
FF = 9216
CACHE = 2048
ROWS = 32
HQ = 6144


def draw_tokens(key, part):
    key = jax.random.fold_in(key, 11)
    keys = jax.random.split(key, 2)
    base = jax.random.truncated_normal(keys[0], -4.0, 4.0, (ROWS, D), jnp.float32)
    rough = jax.random.uniform(keys[1], (D,), jnp.float32, 0.5, 1.5)
    place = jnp.arange(D, dtype=jnp.float32) / D
    column_scale = 3.0 ** place * rough
    values = base * column_scale[None, :]
    return values.astype(jnp.bfloat16)


def draw_key_cache(key, part):
    key = jax.random.fold_in(key, 23)
    keys = jax.random.split(key, 1)
    base = 2.0 * jax.random.truncated_normal(keys[0], -4.0, 4.0, (ROWS, CACHE, HEAD), jnp.float32)
    values = base
    return values.astype(jnp.bfloat16)


def draw_lengths(key, part):
    key = jax.random.fold_in(key, 37)
    keys = jax.random.split(key, 2)
    drawn = jax.random.randint(keys[0], (ROWS,), 2, CACHE + 1, jnp.int32)
    full_row = jax.random.randint(keys[1], (), 0, ROWS, jnp.int32)
    return jnp.where(jnp.arange(ROWS, dtype=jnp.int32) == full_row, CACHE, drawn).astype(jnp.int32)


def level_of(stream_key, shape, cuts, least, high):
    level = 1.0
    for dim, parts in cuts:
        steps = jax.random.uniform(jax.random.fold_in(jax.random.fold_in(stream_key, 6), dim), (parts,), jnp.float32, least / len(cuts), high / len(cuts))
        level = level * jnp.repeat(jnp.exp(steps), shape[dim] // parts).reshape((-1,) + (1,) * (len(shape) - 1 - dim))
    return level


def gaussian(key, dims, scale, reach, pieces=(), held_as=jnp.bfloat16):
    loudness = level_of(key, dims, pieces, -0.22, 0.18) if pieces else 1.0
    values = jax.random.normal(key, dims, jnp.float32) * scale * loudness
    return jnp.minimum(jnp.maximum(values, -reach), reach).astype(held_as)


def setup_inputs(seed: int = 0, part: int = 0) -> dict:
    key_list = jax.random.split(jax.random.key(seed), 10)
    own_keys = jax.random.split(jax.random.fold_in(key_list[9], part), 10)
    return {
        "tokens": draw_tokens(jax.random.fold_in(jax.random.fold_in(key_list[9], part), 71), part),
        "w_query": gaussian(key_list[1], (D, HQ), D ** -0.5, 0.046875, ((0, 2), (1, 8))),
        "w_keyval": gaussian(key_list[2], (D, 2 * HEAD), D ** -0.5, 0.046875, ((0, 2), (1, 8))),
        "w_inner": gaussian(key_list[3], (D, FF), D ** -0.5, 0.046875, ((0, 2), (1, 8))),
        "w_outer": gaussian(key_list[4], (FF, D), FF ** -0.5, 0.0625, ((0, 8), (1, 2))),
        "w_attn_out": gaussian(key_list[5], (HQ, D), (HQ // 32) ** -0.5, 0.4375, ((0, 8), (1, 2))),
        "key_cache": draw_key_cache(jax.random.fold_in(jax.random.fold_in(key_list[9], part), 71), part),
        "value_cache": gaussian(own_keys[7], (ROWS, CACHE, HEAD), 1.0, 6.0, ((0, 16),)),
        "lengths": draw_lengths(jax.random.fold_in(jax.random.fold_in(key_list[9], part), 71), part),
    }


def attend_row(items):
    query, keys, values, length, new_key, new_value = items
    scale = 1.0 / HEAD ** 0.5
    qf = query.astype(jnp.float32)
    scores = jnp.einsum('hd,sd->hs', qf, keys.astype(jnp.float32)) * scale
    valid = jnp.arange(CACHE, dtype=jnp.int32)[None, :] < length
    self_score = lax.optimization_barrier(jnp.sum(qf * new_key.astype(jnp.float32)[None, :], axis=1)) * scale
    masked = jnp.where(valid, scores, -jnp.inf)
    top = jnp.maximum(lax.optimization_barrier(jnp.max(masked, axis=1)), self_score)
    cached = jnp.where(valid, jnp.exp(masked - top[:, None]), 0.0)
    own = jnp.exp(self_score - top)
    total = lax.optimization_barrier(jnp.sum(cached, axis=1)) + own
    cached_w = (cached / total[:, None]).astype(jnp.bfloat16)
    own_w = (own / total).astype(jnp.bfloat16)
    result = jnp.einsum('hs,sd->hd', cached_w.astype(jnp.float32), values.astype(jnp.float32))
    result = result + own_w.astype(jnp.float32)[:, None] * new_value.astype(jnp.float32)[None, :]
    return result.astype(jnp.bfloat16).reshape(HQ)

def reference(tokens, w_query, w_keyval, w_inner, w_outer, w_attn_out, key_cache, value_cache, lengths):
    x = tokens.astype(jnp.float32)
    mean = lax.optimization_barrier(jnp.sum(x, axis=1)) / D
    var = lax.optimization_barrier(jnp.sum(x * x, axis=1)) / D - mean * mean
    normed = ((x - mean[:, None]) * lax.rsqrt(var + 1e-05)[:, None]).astype(jnp.bfloat16)
    query = jnp.dot(normed, w_query, preferred_element_type=jnp.float32).astype(jnp.bfloat16)
    keyval = jnp.dot(normed, w_keyval, preferred_element_type=jnp.float32).astype(jnp.bfloat16)
    new_key = keyval[:, :HEAD]
    new_value = keyval[:, HEAD:]
    attended = lax.map(attend_row, (query.reshape(ROWS, HEADS, HEAD), key_cache, value_cache, lengths, new_key, new_value))
    hidden = jax.nn.gelu(jnp.dot(normed, w_inner, preferred_element_type=jnp.float32), approximate=True).astype(jnp.bfloat16)
    branch = jnp.dot(attended, w_attn_out, preferred_element_type=jnp.float32) + jnp.dot(hidden, w_outer, preferred_element_type=jnp.float32)
    return (x + branch).astype(jnp.bfloat16)
```

```python
import jax
import jax.numpy as jnp
from jax import lax
from jax.sharding import PartitionSpec as P

D = 18432
HEAD = 256


def attend_block(query, key_cache, value_cache, lengths, new_key, new_value):
    scale = 1.0 / HEAD**0.5
    scores = (
        jnp.einsum("rhd,rsd->rhs", query, key_cache, preferred_element_type=jnp.float32) * scale
    )
    positions = lax.broadcasted_iota(jnp.int32, (1, 1, key_cache.shape[1]), 2)
    valid = positions < lengths[:, None, None]
    self_score = (
        jnp.einsum("rhd,rd->rh", query, new_key, preferred_element_type=jnp.float32) * scale
    )
    masked = jnp.where(valid, scores, -jnp.inf)
    top = jnp.maximum(jnp.max(masked, axis=2), self_score)
    cached = jnp.where(valid, jnp.exp(masked - top[:, :, None]), 0.0)
    own = jnp.exp(self_score - top)
    total = jnp.sum(cached, axis=2) + own
    cached_w = (cached / total[:, :, None]).astype(jnp.bfloat16)
    own_w = (own / total).astype(jnp.bfloat16)
    result = jnp.einsum("rhs,rsd->rhd", cached_w, value_cache, preferred_element_type=jnp.float32)
    result = (
        result + own_w.astype(jnp.float32)[:, :, None] * new_value.astype(jnp.float32)[:, None, :]
    )
    return result.astype(jnp.bfloat16).reshape(query.shape[0], query.shape[1] * query.shape[2])


def body(tokens, w_query, w_keyval, w_inner, w_outer, w_attn_out, key_cache, value_cache, lengths):
    x = tokens.astype(jnp.float32)
    moment_one, moment_two = lax.psum((jnp.sum(x, axis=1), jnp.sum(x * x, axis=1)), "yz")
    mean = moment_one / D
    var = moment_two / D - mean * mean
    normed_local = ((x - mean[:, None]) * lax.rsqrt(var + 1e-05)[:, None]).astype(jnp.bfloat16)
    n = lax.axis_size("gx")
    copies = jnp.broadcast_to(normed_local[None], (n,) + normed_local.shape)
    normed = lax.all_to_all(copies, "gx", split_axis=0, concat_axis=0, tiled=True).reshape(
        n * normed_local.shape[0], normed_local.shape[1]
    )
    query_part = jnp.dot(normed, w_query, preferred_element_type=jnp.float32)
    keyval_part = jnp.dot(normed, w_keyval, preferred_element_type=jnp.float32)
    query_rows, keyval_rows = (
        lax.all_to_all(query_part, "gx", split_axis=0, concat_axis=1, tiled=True),
        lax.all_to_all(keyval_part, "gx", split_axis=0, concat_axis=1, tiled=True),
    )
    query_sum, keyval_sum = (
        lax.psum_scatter(query_rows, "yz", scatter_dimension=0, tiled=True),
        lax.psum_scatter(keyval_rows, "yz", scatter_dimension=0, tiled=True),
    )
    inner_part = jnp.dot(normed, w_inner, preferred_element_type=jnp.float32)
    inner_total = inner_part + lax.ppermute(inner_part, "yz", [(0, 1), (1, 0)])
    hidden = jax.nn.gelu(inner_total, approximate=True).astype(jnp.bfloat16)
    local_rows = query_sum.shape[0]
    query = query_sum.astype(jnp.bfloat16).reshape(local_rows, query_sum.shape[1] // HEAD, HEAD)
    keyval = keyval_sum.astype(jnp.bfloat16)
    attended = attend_block(
        query, key_cache, value_cache, lengths, keyval[:, :HEAD], keyval[:, HEAD:]
    )
    paired_rows = lax.all_gather(attended, "yz", axis=0, tiled=True)
    attended_cols = lax.all_to_all(paired_rows, "gx", split_axis=1, concat_axis=0, tiled=True)
    part = jnp.dot(attended_cols, w_attn_out, preferred_element_type=jnp.float32) + jnp.dot(
        hidden, w_outer, preferred_element_type=jnp.float32
    )
    pieces = part.astype(jnp.bfloat16).reshape(n, x.shape[0], x.shape[1])
    pieces = lax.all_to_all(pieces, "gx", split_axis=0, concat_axis=0, tiled=True)
    branch = jnp.sum(pieces.astype(jnp.float32), axis=0)
    return (x + branch).astype(jnp.bfloat16)


def solution(mesh):
    in_specs = (
        P(("groups", "gx"), "yz"),
        P("yz", "gx"),
        P("yz", "gx"),
        P("yz", "gx"),
        P("gx", "yz"),
        P("gx", "yz"),
        P(("groups", "gx", "yz"), None, None),
        P(("groups", "gx", "yz"), None, None),
        P(("groups", "gx", "yz")),
    )
    out_specs = P(("groups", "gx"), "yz")
    return jax.shard_map(body, mesh=mesh, in_specs=in_specs, out_specs=out_specs, check_vma=False)
```

```python
import functools

import jax
import jax.numpy as jnp
from jax import lax
from jax.experimental import pallas as pl
from jax.experimental.pallas import tpu as pltpu
from jax.sharding import PartitionSpec as P

D = 18432
HEAD = 256


def attend_block(query, key_cache, value_cache, lengths, new_key, new_value):
    scale = 1.0 / HEAD**0.5
    scores = (
        jnp.einsum("rhd,rsd->rhs", query, key_cache, preferred_element_type=jnp.float32) * scale
    )
    positions = lax.broadcasted_iota(jnp.int32, (1, 1, key_cache.shape[1]), 2)
    valid = positions < lengths[:, None, None]
    self_score = (
        jnp.einsum("rhd,rd->rh", query, new_key, preferred_element_type=jnp.float32) * scale
    )
    masked = jnp.where(valid, scores, -jnp.inf)
    top = jnp.maximum(jnp.max(masked, axis=2), self_score)
    cached = jnp.where(valid, jnp.exp(masked - top[:, :, None]), 0.0)
    own = jnp.exp(self_score - top)
    total = jnp.sum(cached, axis=2) + own
    cached_w = (cached / total[:, :, None]).astype(jnp.bfloat16)
    own_w = (own / total).astype(jnp.bfloat16)
    result = jnp.einsum("rhs,rsd->rhd", cached_w, value_cache, preferred_element_type=jnp.float32)
    result = (
        result + own_w.astype(jnp.float32)[:, :, None] * new_value.astype(jnp.float32)[:, None, :]
    )
    return result.astype(jnp.bfloat16).reshape(query.shape[0], query.shape[1] * query.shape[2])


def body(tokens, w_query, w_keyval, w_inner, w_outer, w_attn_out, key_cache, value_cache, lengths):
    x = tokens.astype(jnp.float32)
    moment_one, moment_two = lax.psum((jnp.sum(x, axis=1), jnp.sum(x * x, axis=1)), "yz")
    mean = moment_one / D
    var = moment_two / D - mean * mean
    normed_local = ((x - mean[:, None]) * lax.rsqrt(var + 1e-05)[:, None]).astype(jnp.bfloat16)
    n = lax.axis_size("gx")
    copies = jnp.broadcast_to(normed_local[None], (n,) + normed_local.shape)
    normed = lax.all_to_all(copies, "gx", split_axis=0, concat_axis=0, tiled=True).reshape(
        n * normed_local.shape[0], normed_local.shape[1]
    )
    query_part = jnp.dot(normed, w_query, preferred_element_type=jnp.float32)
    keyval_part = jnp.dot(normed, w_keyval, preferred_element_type=jnp.float32)
    query_rows, keyval_rows = (
        lax.all_to_all(query_part, "gx", split_axis=0, concat_axis=1, tiled=True),
        lax.all_to_all(keyval_part, "gx", split_axis=0, concat_axis=1, tiled=True),
    )
    query_sum, keyval_sum = (
        lax.psum_scatter(query_rows, "yz", scatter_dimension=0, tiled=True),
        lax.psum_scatter(keyval_rows, "yz", scatter_dimension=0, tiled=True),
    )
    inner_part = jnp.dot(normed, w_inner, preferred_element_type=jnp.float32)
    inner_total = inner_part + lax.ppermute(inner_part, "yz", [(0, 1), (1, 0)])
    hidden = jax.nn.gelu(inner_total, approximate=True).astype(jnp.bfloat16)
    local_rows = query_sum.shape[0]
    query = query_sum.astype(jnp.bfloat16).reshape(local_rows, query_sum.shape[1] // HEAD, HEAD)
    keyval = keyval_sum.astype(jnp.bfloat16)
    attended = attend_block(
        query, key_cache, value_cache, lengths, keyval[:, :HEAD], keyval[:, HEAD:]
    )
    paired_rows = lax.all_gather(attended, "yz", axis=0, tiled=True)
    attended_cols = lax.all_to_all(paired_rows, "gx", split_axis=1, concat_axis=0, tiled=True)
    part = jnp.dot(attended_cols, w_attn_out, preferred_element_type=jnp.float32) + jnp.dot(
        hidden, w_outer, preferred_element_type=jnp.float32
    )
    pieces = part.astype(jnp.bfloat16).reshape(n, x.shape[0], x.shape[1])
    pieces = lax.all_to_all(pieces, "gx", split_axis=0, concat_axis=0, tiled=True)
    branch = jnp.sum(pieces.astype(jnp.float32), axis=0)
    return (x + branch).astype(jnp.bfloat16)


def gelu(x):
    c = 0.7978845608028654
    return 0.5 * x * (1.0 + jnp.tanh(c * (x + 0.044715 * (x * x * x))))


def block_kernel(
    n, tok, wq, wkv, wi, wo, wa, kc, vc, lens, out,
    buf_q, buf_i, buf_a, buf_kv, kbuf, vbuf, xf, xb, nbuf, bsend, brecv,
    mom, mom_in, acc_q, half_in, qsend, qrecv, qs, acc_i, inner_in, hb,
    asend, arecv, ahalf, ahalf_in,
    sem_q, sem_i, sem_o, sem_a, sem_l, pair_send, pair_recv, gx_send, gx_recv, b_send, b_recv,
):
    g = lax.axis_index("gx")
    y = lax.axis_index("yz")
    rows, width = tok.shape
    half = rows // 2
    hrows = n * half
    cq, cols = buf_q.shape[0], buf_q.shape[2]
    ci, inner = buf_i.shape[0], buf_i.shape[2]
    per = cols // HEAD
    groups = b_send.shape[0]
    wide = width // groups

    def load_q(i):
        return pltpu.make_async_copy(wq.at[pl.ds(i * cols, cols), :], buf_q.at[i], sem_q.at[i])

    def load_i(i):
        return pltpu.make_async_copy(wi.at[pl.ds(i * inner, inner), :], buf_i.at[i], sem_i.at[i])

    def load_o(i):
        return pltpu.make_async_copy(wo.at[:, pl.ds(i * inner, inner)], buf_i.at[i], sem_o.at[i])

    def load_a(i):
        return pltpu.make_async_copy(wa.at[:, pl.ds(i * cols, cols)], buf_a.at[i], sem_a.at[i])

    load_kv = pltpu.make_async_copy(wkv, buf_kv, sem_l.at[0])
    load_k = pltpu.make_async_copy(kc, kbuf, sem_l.at[1])
    load_v = pltpu.make_async_copy(vc, vbuf, sem_l.at[2])

    def each(count, do):
        def step(i, c):
            do(i)
            return c

        lax.fori_loop(0, count, step, 0)

    each(cq, lambda i: load_q(i).start())
    load_kv.start()
    each(ci, lambda i: load_i(i).start())
    load_k.start()
    load_v.start()
    each(cq, lambda i: load_a(i).start())

    barrier = pltpu.get_barrier_semaphore()
    for i in range(1, n):
        pl.semaphore_signal(
            barrier, inc=1, device_id={"gx": lax.rem(g + i, n)}, device_id_type=pl.DeviceIdType.MESH
        )
    pl.semaphore_signal(barrier, inc=1, device_id={"yz": 1 - y}, device_id_type=pl.DeviceIdType.MESH)

    def to_pair(src, dst, k):
        return pltpu.make_async_remote_copy(
            src_ref=src, dst_ref=dst, send_sem=pair_send.at[k], recv_sem=pair_recv.at[k],
            device_id={"yz": 1 - y}, device_id_type=pl.DeviceIdType.MESH,
        )

    def to_gx(src, dst, send, recv, i):
        return pltpu.make_async_remote_copy(
            src_ref=src, dst_ref=dst, send_sem=send, recv_sem=recv,
            device_id={"gx": lax.rem(g + i, n)}, device_id_type=pl.DeviceIdType.MESH,
        )

    x = tok[...].astype(jnp.float32)
    mom[0:rows, :] = jnp.broadcast_to(jnp.sum(x, axis=1, keepdims=True), (rows, 128))
    mom[rows : 2 * rows, :] = jnp.broadcast_to(jnp.sum(x * x, axis=1, keepdims=True), (rows, 128))
    pl.semaphore_wait(barrier, n)
    exchange = to_pair(mom, mom_in, 0)
    exchange.start()
    exchange.wait()
    both = mom[...] + mom_in[...]
    mean = both[0:rows, 0:1] / D
    var = both[rows : 2 * rows, 0:1] / D - mean * mean
    nbuf[g] = ((x - mean) * lax.rsqrt(var + 1e-05)).astype(jnp.bfloat16)

    gathers = [to_gx(nbuf.at[g], nbuf.at[g], gx_send.at[0, i - 1], gx_recv.at[0, i - 1], i) for i in range(1, n)]
    for c in gathers:
        c.start()
    for c in gathers:
        c.wait()
    for s in range(n):
        v = nbuf[s].astype(jnp.float32)
        xf[s * half : (s + 1) * half, :] = v[0:half, :]
        xf[hrows + s * half : hrows + (s + 1) * half, :] = v[half:rows, :]
    xb[...] = xf[...].astype(jnp.bfloat16)

    acc_q[...] = jnp.zeros_like(acc_q)

    def q_step(i):
        load_q(i).wait()
        acc_q[:, 0:cols] += jnp.dot(
            xb[:, pl.ds(pl.multiple_of(i * cols, 128), cols)], buf_q[i],
            preferred_element_type=jnp.float32,
        )

    each(cq, q_step)
    load_kv.wait()
    kv = jnp.dot(xb[...], buf_kv[...], preferred_element_type=jnp.float32)
    kvw = kv.shape[1]
    spread = 128 // kvw
    kv = jnp.concatenate([kv] * spread, axis=1)
    lane = lax.broadcasted_iota(jnp.int32, kv.shape, 1) // kvw
    acc_q[:, cols : cols + 128] = jnp.where(lane == lax.rem(g, spread), kv, 0.0)

    exchange = to_pair(acc_q.at[pl.ds(pl.multiple_of((1 - y) * hrows, 16), hrows), :], half_in, 1)
    exchange.start()
    exchange.wait()
    mine = acc_q[pl.ds(pl.multiple_of(y * hrows, 16), hrows), :] + half_in[...]
    mine = mine.astype(jnp.bfloat16).astype(jnp.float32)
    for s in range(n):
        qsend[s] = mine[s * half : (s + 1) * half, :]
    q_copies = [
        to_gx(qsend.at[lax.rem(g + i, n)], qrecv.at[g], gx_send.at[1, i - 1], gx_recv.at[1, i - 1], i)
        for i in range(1, n)
    ]
    for c in q_copies:
        c.start()
    qrecv[g] = qsend[g]

    acc_i[...] = jnp.zeros_like(acc_i)

    def i_step(i):
        load_i(i).wait()
        acc_i[...] += jnp.dot(
            xb[:, pl.ds(pl.multiple_of(i * inner, 128), inner)], buf_i[i],
            preferred_element_type=jnp.float32,
        )
        load_o(i).start()

    each(ci, i_step)
    inner_copy = to_pair(acc_i, inner_in, 2)
    inner_copy.start()

    for c in q_copies:
        c.wait()
    load_k.wait()
    load_v.wait()
    scale = 1.0 / HEAD**0.5
    for j in range(half):
        for s in range(n):
            for h in range(per):
                qs[j, s * per + h : s * per + h + 1, :] = qrecv[s, j : j + 1, h * HEAD : (h + 1) * HEAD]
        tails = [qrecv[s, j : j + 1, cols : cols + 128] for s in range(n)]
        lanes = [sum(tails[t * spread + 1 : (t + 1) * spread], tails[t * spread]) for t in range(n // spread)]
        new = jnp.concatenate(lanes, axis=1)
        new_key, new_value = new[:, :HEAD], new[:, HEAD:]
        q = qs[j]
        scores = lax.dot_general(
            q.astype(jnp.bfloat16), kbuf[j], (((1,), (1,)), ((), ())),
            preferred_element_type=jnp.float32,
        ) * scale
        valid = lax.broadcasted_iota(jnp.int32, scores.shape, 1) < lens[j]
        self_score = jnp.sum(q * new_key, axis=1, keepdims=True) * scale
        masked = jnp.where(valid, scores, -jnp.inf)
        top = jnp.maximum(jnp.max(masked, axis=1, keepdims=True), self_score)
        cached = jnp.where(valid, jnp.exp(masked - top), 0.0)
        own = jnp.exp(self_score - top)
        total = jnp.sum(cached, axis=1, keepdims=True) + own
        weights = (cached / total).astype(jnp.bfloat16)
        own_w = (own / total).astype(jnp.bfloat16).astype(jnp.float32)
        res = jnp.dot(weights, vbuf[j], preferred_element_type=jnp.float32) + own_w * new_value
        res = res.astype(jnp.bfloat16).astype(jnp.float32)
        for s in range(n):
            for h in range(per):
                asend[s, j : j + 1, h * HEAD : (h + 1) * HEAD] = res[s * per + h : s * per + h + 1, :]
    a_copies = [
        to_gx(asend.at[lax.rem(g + i, n)], arecv.at[g], gx_send.at[2, i - 1], gx_recv.at[2, i - 1], i)
        for i in range(1, n)
    ]
    for c in a_copies:
        c.start()
    arecv[g] = asend[g]

    inner_copy.wait()
    hb[...] = gelu(acc_i[...] + inner_in[...]).astype(jnp.bfloat16)

    def o_step(i):
        load_o(i).wait()
        xf[:, pl.ds(pl.multiple_of(i * inner, 128), inner)] = jnp.dot(
            hb[...], buf_i[i], preferred_element_type=jnp.float32
        )

    first = ci // 2

    def o_second(i):
        o_step(i + first)

    each(first, o_step)
    for c in a_copies:
        c.wait()
    for s in range(n):
        ahalf[s * half : (s + 1) * half, :] = arecv[s]
    exchange = to_pair(ahalf, ahalf_in, 3)
    exchange.start()
    each(ci - first, o_second)
    exchange.wait()
    a_own, a_other = ahalf[...], ahalf_in[...]
    low = jnp.where(y == 0, a_own, a_other)
    high = jnp.where(y == 0, a_other, a_own)
    att = jnp.concatenate([low, high], axis=0).astype(jnp.bfloat16)
    acc_q[:, 0:cols] = att.astype(jnp.float32)

    def b_copy(k, i):
        at = pl.ds(pl.multiple_of(k * wide, 128), wide)
        return to_gx(
            bsend.at[lax.rem(g + i, n), :, at], brecv.at[g, :, at],
            b_send.at[k, i - 1], b_recv.at[k, i - 1], i,
        )

    chunks = wide // cols

    def b_step(k):
        a = acc_q[:, 0:cols].astype(jnp.bfloat16)
        for t in range(chunks):
            m = k * chunks + t
            load_a(m).wait()
            at = pl.ds(pl.multiple_of(m * cols, 128), cols)
            r = xf[:, at] + jnp.dot(a, buf_a[m], preferred_element_type=jnp.float32)
            for s in range(n):
                piece = jnp.concatenate(
                    [r[s * half : (s + 1) * half, :], r[hrows + s * half : hrows + (s + 1) * half, :]],
                    axis=0,
                )
                bsend[s, :, at] = piece.astype(jnp.bfloat16)
        for i in range(1, n):
            b_copy(k, i).start()

    each(groups, b_step)
    brecv[g] = bsend[g]

    def end_step(k):
        for i in range(1, n):
            b_copy(k, i).wait()
        at = pl.ds(pl.multiple_of(k * wide, 128), wide)
        total = brecv[0, :, at].astype(jnp.float32)
        for s in range(1, n):
            total += brecv[s, :, at].astype(jnp.float32)
        out[:, at] = (tok[:, at].astype(jnp.float32) + total).astype(jnp.bfloat16)

    each(groups, end_step)


def fused(n, tokens, w_query, w_keyval, w_inner, w_outer, w_attn_out, key_cache, value_cache, lengths):
    rows, width = tokens.shape
    cols, inner, kvw = w_query.shape[1], w_inner.shape[1], w_keyval.shape[1]
    cq, ci = width // cols, width // inner
    half = rows // 2
    all_rows, hrows = n * rows, n * half
    groups = 4 if cq % 4 == 0 else 1
    heads = n * cols // HEAD
    bf, f32 = jnp.bfloat16, jnp.float32
    V, dma = pltpu.VMEM, pltpu.SemaphoreType.DMA
    vmem = pl.BlockSpec(memory_space=pltpu.VMEM)
    hbm = pl.BlockSpec(memory_space=pl.ANY)
    return pl.pallas_call(
        functools.partial(block_kernel, n),
        out_shape=jax.ShapeDtypeStruct(tokens.shape, bf),
        in_specs=[vmem] + [hbm] * 7 + [pl.BlockSpec(memory_space=pltpu.SMEM)],
        out_specs=vmem,
        scratch_shapes=[
            V((cq, cols, cols), bf),
            V((ci, inner, inner), bf),
            V((cq, cols, cols), bf),
            V((width, kvw), bf),
            V(key_cache.shape, bf),
            V(value_cache.shape, bf),
            V((all_rows, width), f32),
            V((all_rows, width), bf),
            V((n, rows, width), bf),
            V((n, rows, width), bf),
            V((n, rows, width), bf),
            V((2 * rows, 128), f32),
            V((2 * rows, 128), f32),
            V((all_rows, cols + 128), f32),
            V((hrows, cols + 128), f32),
            V((n, half, cols + 128), f32),
            V((n, half, cols + 128), f32),
            V((half, heads, HEAD), f32),
            V((all_rows, inner), f32),
            V((all_rows, inner), f32),
            V((all_rows, inner), bf),
            V((n, half, cols), f32),
            V((n, half, cols), f32),
            V((hrows, cols), f32),
            V((hrows, cols), f32),
            dma((cq,)),
            dma((ci,)),
            dma((ci,)),
            dma((cq,)),
            dma((3,)),
            dma((4,)),
            dma((4,)),
            dma((3, n - 1)),
            dma((3, n - 1)),
            dma((groups, n - 1)),
            dma((groups, n - 1)),
        ],
        compiler_params=pltpu.CompilerParams(
            collective_id=0, has_side_effects=True, vmem_limit_bytes=62 * 1024 * 1024
        ),
    )(tokens, w_query, w_keyval, w_inner, w_outer, w_attn_out, key_cache, value_cache, lengths)


def plan(n):
    def run(tokens, w_query, w_keyval, w_inner, *rest):
        width, cols, inner = tokens.shape[1], w_query.shape[1], w_inner.shape[1]
        fits = (
            cols % HEAD == 0 and inner % 128 == 0 and width % cols == 0 and width % inner == 0
            and 128 % w_keyval.shape[1] == 0 and tokens.shape[0] == 4 and n * 2 % 16 == 0
        )
        args = (tokens, w_query, w_keyval, w_inner) + rest
        return fused(n, *args) if fits else body(*args)

    return run


def solution(mesh):
    in_specs = (
        P(("groups", "gx"), "yz"),
        P("yz", "gx"),
        P("yz", "gx"),
        P("yz", "gx"),
        P("gx", "yz"),
        P("gx", "yz"),
        P(("groups", "gx", "yz"), None, None),
        P(("groups", "gx", "yz"), None, None),
        P(("groups", "gx", "yz")),
    )
    out_specs = P(("groups", "gx"), "yz")
    return jax.shard_map(plan(mesh.shape["gx"]), mesh=mesh, in_specs=in_specs, out_specs=out_specs, check_vma=False)
```

```python
import functools

import jax
import jax.numpy as jnp
from jax import lax
from jax.experimental import pallas as pl
from jax.experimental.pallas import tpu as pltpu
from jax.sharding import PartitionSpec as P

D = 18432
HEAD = 256


def attend_block(query, key_cache, value_cache, lengths, new_key, new_value):
    scale = 1.0 / HEAD**0.5
    scores = (
        jnp.einsum("rhd,rsd->rhs", query, key_cache, preferred_element_type=jnp.float32) * scale
    )
    positions = lax.broadcasted_iota(jnp.int32, (1, 1, key_cache.shape[1]), 2)
    valid = positions < lengths[:, None, None]
    self_score = (
        jnp.einsum("rhd,rd->rh", query, new_key, preferred_element_type=jnp.float32) * scale
    )
    masked = jnp.where(valid, scores, -jnp.inf)
    top = jnp.maximum(jnp.max(masked, axis=2), self_score)
    cached = jnp.where(valid, jnp.exp(masked - top[:, :, None]), 0.0)
    own = jnp.exp(self_score - top)
    total = jnp.sum(cached, axis=2) + own
    cached_w = (cached / total[:, :, None]).astype(jnp.bfloat16)
    own_w = (own / total).astype(jnp.bfloat16)
    result = jnp.einsum("rhs,rsd->rhd", cached_w, value_cache, preferred_element_type=jnp.float32)
    result = (
        result + own_w.astype(jnp.float32)[:, :, None] * new_value.astype(jnp.float32)[:, None, :]
    )
    return result.astype(jnp.bfloat16).reshape(query.shape[0], query.shape[1] * query.shape[2])


def body(tokens, w_query, w_keyval, w_inner, w_outer, w_attn_out, key_cache, value_cache, lengths):
    x = tokens.astype(jnp.float32)
    moment_one, moment_two = lax.psum((jnp.sum(x, axis=1), jnp.sum(x * x, axis=1)), "yz")
    mean = moment_one / D
    var = moment_two / D - mean * mean
    normed_local = ((x - mean[:, None]) * lax.rsqrt(var + 1e-05)[:, None]).astype(jnp.bfloat16)
    n = lax.axis_size("gx")
    copies = jnp.broadcast_to(normed_local[None], (n,) + normed_local.shape)
    normed = lax.all_to_all(copies, "gx", split_axis=0, concat_axis=0, tiled=True).reshape(
        n * normed_local.shape[0], normed_local.shape[1]
    )
    query_part = jnp.dot(normed, w_query, preferred_element_type=jnp.float32)
    keyval_part = jnp.dot(normed, w_keyval, preferred_element_type=jnp.float32)
    query_rows, keyval_rows = (
        lax.all_to_all(query_part, "gx", split_axis=0, concat_axis=1, tiled=True),
        lax.all_to_all(keyval_part, "gx", split_axis=0, concat_axis=1, tiled=True),
    )
    query_sum, keyval_sum = (
        lax.psum_scatter(query_rows, "yz", scatter_dimension=0, tiled=True),
        lax.psum_scatter(keyval_rows, "yz", scatter_dimension=0, tiled=True),
    )
    inner_part = jnp.dot(normed, w_inner, preferred_element_type=jnp.float32)
    inner_total = inner_part + lax.ppermute(inner_part, "yz", [(0, 1), (1, 0)])
    hidden = jax.nn.gelu(inner_total, approximate=True).astype(jnp.bfloat16)
    local_rows = query_sum.shape[0]
    query = query_sum.astype(jnp.bfloat16).reshape(local_rows, query_sum.shape[1] // HEAD, HEAD)
    keyval = keyval_sum.astype(jnp.bfloat16)
    attended = attend_block(
        query, key_cache, value_cache, lengths, keyval[:, :HEAD], keyval[:, HEAD:]
    )
    paired_rows = lax.all_gather(attended, "yz", axis=0, tiled=True)
    attended_cols = lax.all_to_all(paired_rows, "gx", split_axis=1, concat_axis=0, tiled=True)
    part = jnp.dot(attended_cols, w_attn_out, preferred_element_type=jnp.float32) + jnp.dot(
        hidden, w_outer, preferred_element_type=jnp.float32
    )
    pieces = part.astype(jnp.bfloat16).reshape(n, x.shape[0], x.shape[1])
    pieces = lax.all_to_all(pieces, "gx", split_axis=0, concat_axis=0, tiled=True)
    branch = jnp.sum(pieces.astype(jnp.float32), axis=0)
    return (x + branch).astype(jnp.bfloat16)


def gelu(x):
    c = 0.7978845608028654
    return 0.5 * x * (1.0 + jnp.tanh(c * (x + 0.044715 * (x * x * x))))


def block_kernel(
    n, tok, wq, wkv, wi, wo, wa, kc, vc, lens, out,
    buf_q, buf_i, buf_a, buf_kv, kbuf, vbuf, xf, xb, nbuf, bsend, xrecv, zsend, zrecv,
    mom, mom_in, acc_q, half_in, qsend, qrecv, qs, acc_i, inner_in, hb,
    asend, arecv, ahalf, ahalf_in,
    sem_q, sem_i, sem_o, sem_a, sem_l, pair_send, pair_recv, gx_send, gx_recv, b_send, b_recv,
):
    g = lax.axis_index("gx")
    y = lax.axis_index("yz")
    zs = n // 2
    zi, side = lax.div(g, 2), lax.rem(g, 2)
    beside = zi * 2 + 1 - side
    rows, width = tok.shape
    half = rows // 2
    hrows = n * half
    cq, cols = buf_q.shape[0], buf_q.shape[2]
    ci, inner = buf_i.shape[0], buf_i.shape[2]
    per = cols // HEAD
    groups = b_send.shape[0]
    wide = width // groups

    def load_q(i):
        return pltpu.make_async_copy(wq.at[pl.ds(i * cols, cols), :], buf_q.at[i], sem_q.at[i])

    def load_i(i):
        return pltpu.make_async_copy(wi.at[pl.ds(i * inner, inner), :], buf_i.at[i], sem_i.at[i])

    def load_o(i):
        return pltpu.make_async_copy(wo.at[:, pl.ds(i * inner, inner)], buf_i.at[i], sem_o.at[i])

    def load_a(i):
        return pltpu.make_async_copy(wa.at[:, pl.ds(i * cols, cols)], buf_a.at[i], sem_a.at[i])

    load_kv = pltpu.make_async_copy(wkv, buf_kv, sem_l.at[0])
    load_k = pltpu.make_async_copy(kc, kbuf, sem_l.at[1])
    load_v = pltpu.make_async_copy(vc, vbuf, sem_l.at[2])

    def each(count, do):
        def step(i, c):
            do(i)
            return c

        lax.fori_loop(0, count, step, 0)

    each(cq, lambda i: load_q(i).start())
    load_kv.start()
    each(ci, lambda i: load_i(i).start())
    load_k.start()
    load_v.start()
    each(cq, lambda i: load_a(i).start())

    barrier = pltpu.get_barrier_semaphore()
    for i in range(1, n):
        pl.semaphore_signal(
            barrier, inc=1, device_id={"gx": lax.rem(g + i, n)}, device_id_type=pl.DeviceIdType.MESH
        )
    pl.semaphore_signal(barrier, inc=1, device_id={"yz": 1 - y}, device_id_type=pl.DeviceIdType.MESH)

    def to_pair(src, dst, k):
        return pltpu.make_async_remote_copy(
            src_ref=src, dst_ref=dst, send_sem=pair_send.at[k], recv_sem=pair_recv.at[k],
            device_id={"yz": 1 - y}, device_id_type=pl.DeviceIdType.MESH,
        )

    def to_gx(src, dst, send, recv, i):
        return pltpu.make_async_remote_copy(
            src_ref=src, dst_ref=dst, send_sem=send, recv_sem=recv,
            device_id={"gx": lax.rem(g + i, n)}, device_id_type=pl.DeviceIdType.MESH,
        )

    def to_row(src, dst, send, recv, peer):
        return pltpu.make_async_remote_copy(
            src_ref=src, dst_ref=dst, send_sem=send, recv_sem=recv,
            device_id={"gx": peer}, device_id_type=pl.DeviceIdType.MESH,
        )

    x = tok[...].astype(jnp.float32)
    mom[0:rows, :] = jnp.broadcast_to(jnp.sum(x, axis=1, keepdims=True), (rows, 128))
    mom[rows : 2 * rows, :] = jnp.broadcast_to(jnp.sum(x * x, axis=1, keepdims=True), (rows, 128))
    pl.semaphore_wait(barrier, n)
    exchange = to_pair(mom, mom_in, 0)
    exchange.start()
    exchange.wait()
    both = mom[...] + mom_in[...]
    mean = both[0:rows, 0:1] / D
    var = both[rows : 2 * rows, 0:1] / D - mean * mean
    nbuf[g] = ((x - mean) * lax.rsqrt(var + 1e-05)).astype(jnp.bfloat16)

    def g_copy(slot, m, peer):
        return to_row(nbuf.at[slot], nbuf.at[slot], gx_send.at[0, m], gx_recv.at[0, m], peer)

    across = g_copy(g, 0, beside)
    along = [g_copy(g, i, lax.rem(zi + i, zs) * 2 + side) for i in range(1, zs)]
    onward = [g_copy(lax.rem(zi + zs - i, zs) * 2 + side, zs - 1 + i, beside) for i in range(1, zs)]
    for c in along:
        c.start()
    across.start()
    for c, d in zip(along, onward):
        c.wait_recv()
        d.start()
    across.wait()
    for c, d in zip(along, onward):
        c.wait_send()
        d.wait()
    for s in range(n):
        v = nbuf[s].astype(jnp.float32)
        xf[s * half : (s + 1) * half, :] = v[0:half, :]
        xf[hrows + s * half : hrows + (s + 1) * half, :] = v[half:rows, :]
    xb[...] = xf[...].astype(jnp.bfloat16)

    acc_q[...] = jnp.zeros_like(acc_q)

    def q_step(i):
        load_q(i).wait()
        acc_q[:, 0:cols] += jnp.dot(
            xb[:, pl.ds(pl.multiple_of(i * cols, 128), cols)], buf_q[i],
            preferred_element_type=jnp.float32,
        )

    each(cq, q_step)
    load_kv.wait()
    kv = lax.dot_general(
        xb[...], buf_kv[...], (((1,), (1,)), ((), ())), preferred_element_type=jnp.float32
    )
    kvw = kv.shape[1]
    spread = 128 // kvw
    kv = jnp.concatenate([kv] * spread, axis=1)
    lane = lax.broadcasted_iota(jnp.int32, kv.shape, 1) // kvw
    acc_q[:, cols : cols + 128] = jnp.where(lane == lax.rem(g, spread), kv, 0.0)

    exchange = to_pair(acc_q.at[pl.ds(pl.multiple_of((1 - y) * hrows, 16), hrows), :], half_in, 1)
    exchange.start()
    exchange.wait()
    mine = acc_q[pl.ds(pl.multiple_of(y * hrows, 16), hrows), :] + half_in[...]
    mine = mine.astype(jnp.bfloat16).astype(jnp.float32)
    for s in range(n):
        qsend[s] = mine[s * half : (s + 1) * half, :]
    q_copies = [
        to_gx(qsend.at[lax.rem(g + i, n)], qrecv.at[g], gx_send.at[1, i - 1], gx_recv.at[1, i - 1], i)
        for i in range(1, n)
    ]
    for c in q_copies:
        c.start()
    qrecv[g] = qsend[g]

    acc_i[...] = jnp.zeros_like(acc_i)

    def i_step(i):
        load_i(i).wait()
        acc_i[...] += jnp.dot(
            xb[:, pl.ds(pl.multiple_of(i * inner, 128), inner)], buf_i[i],
            preferred_element_type=jnp.float32,
        )
        load_o(i).start()

    each(ci, i_step)
    inner_copy = to_pair(acc_i, inner_in, 2)
    inner_copy.start()

    for c in q_copies:
        c.wait()
    load_k.wait()
    load_v.wait()
    scale = 1.0 / HEAD**0.5
    for j in range(half):
        for s in range(n):
            for h in range(per):
                qs[j, s * per + h : s * per + h + 1, :] = qrecv[s, j : j + 1, h * HEAD : (h + 1) * HEAD]
        tails = [qrecv[s, j : j + 1, cols : cols + 128] for s in range(n)]
        lanes = [sum(tails[t * spread + 1 : (t + 1) * spread], tails[t * spread]) for t in range(n // spread)]
        new = jnp.concatenate(lanes, axis=1)
        new_key, new_value = new[:, :HEAD], new[:, HEAD:]
        q = qs[j]
        scores = lax.dot_general(
            q.astype(jnp.bfloat16), kbuf[j], (((1,), (1,)), ((), ())),
            preferred_element_type=jnp.float32,
        ) * scale
        valid = lax.broadcasted_iota(jnp.int32, scores.shape, 1) < lens[j]
        self_score = jnp.sum(q * new_key, axis=1, keepdims=True) * scale
        masked = jnp.where(valid, scores, -jnp.inf)
        top = jnp.maximum(jnp.max(masked, axis=1, keepdims=True), self_score)
        cached = jnp.where(valid, jnp.exp(masked - top), 0.0)
        own = jnp.exp(self_score - top)
        total = jnp.sum(cached, axis=1, keepdims=True) + own
        weights = (cached / total).astype(jnp.bfloat16)
        own_w = (own / total).astype(jnp.bfloat16).astype(jnp.float32)
        res = jnp.dot(weights, vbuf[j], preferred_element_type=jnp.float32) + own_w * new_value
        res = res.astype(jnp.bfloat16).astype(jnp.float32)
        for s in range(n):
            for h in range(per):
                asend[s, j : j + 1, h * HEAD : (h + 1) * HEAD] = res[s * per + h : s * per + h + 1, :]
    a_copies = [
        to_gx(asend.at[lax.rem(g + i, n)], arecv.at[g], gx_send.at[2, i - 1], gx_recv.at[2, i - 1], i)
        for i in range(1, n)
    ]
    for c in a_copies:
        c.start()
    arecv[g] = asend[g]

    inner_copy.wait()
    hb[...] = gelu(acc_i[...] + inner_in[...]).astype(jnp.bfloat16)

    def o_step(i):
        load_o(i).wait()
        xf[:, pl.ds(pl.multiple_of(i * inner, 128), inner)] = jnp.dot(
            hb[...], buf_i[i], preferred_element_type=jnp.float32
        )

    first = ci // 2

    def o_second(i):
        o_step(i + first)

    each(first, o_step)
    for c in a_copies:
        c.wait()
    for s in range(n):
        ahalf[s * half : (s + 1) * half, :] = arecv[s]
    exchange = to_pair(ahalf, ahalf_in, 3)
    exchange.start()
    each(ci - first, o_second)
    exchange.wait()
    a_own, a_other = ahalf[...], ahalf_in[...]
    low = jnp.where(y == 0, a_own, a_other)
    high = jnp.where(y == 0, a_other, a_own)
    att = jnp.concatenate([low, high], axis=0).astype(jnp.bfloat16)
    acc_q[:, 0:cols] = att.astype(jnp.float32)

    def span(k):
        return pl.ds(k * wide if isinstance(k, int) else pl.multiple_of(k * wide, 128), wide)

    def x_copy(k):
        return to_row(
            bsend.at[1 - side, :, :, span(k)], xrecv.at[:, :, span(k)],
            b_send.at[k, 0], b_recv.at[k, 0], beside,
        )

    def z_copy(k, i):
        z = lax.rem(zi + i, zs)
        return to_row(
            zsend.at[z, :, span(k)], zrecv.at[zi, :, span(k)],
            b_send.at[k, i], b_recv.at[k, i], z * 2 + side,
        )

    def sum_x(k):
        x_copy(k).wait()
        for z in range(zs):
            v = bsend[side, z, :, span(k)].astype(jnp.float32) + xrecv[z, :, span(k)].astype(jnp.float32)
            zsend[z, :, span(k)] = v.astype(jnp.bfloat16)
        for i in range(1, zs):
            z_copy(k, i).start()

    chunks = wide // cols

    def b_step(k):
        a = acc_q[:, 0:cols].astype(jnp.bfloat16)
        for t in range(chunks):
            m = k * chunks + t
            load_a(m).wait()
            at = pl.ds(m * cols if isinstance(m, int) else pl.multiple_of(m * cols, 128), cols)
            r = xf[:, at] + jnp.dot(a, buf_a[m], preferred_element_type=jnp.float32)
            for s in range(n):
                piece = jnp.concatenate(
                    [r[s * half : (s + 1) * half, :], r[hrows + s * half : hrows + (s + 1) * half, :]],
                    axis=0,
                )
                bsend[s % 2, s // 2, :, at] = piece.astype(jnp.bfloat16)
        x_copy(k).start()

    def b_next(k):
        b_step(k + 1)
        sum_x(k)

    b_step(0)
    each(groups - 1, b_next)
    sum_x(groups - 1)
    zrecv[zi] = zsend[zi]

    def end_step(k):
        for i in range(1, zs):
            z_copy(k, i).wait()
        at = span(k)
        total = zrecv[0, :, at].astype(jnp.float32)
        for z in range(1, zs):
            total += zrecv[z, :, at].astype(jnp.float32)
        out[:, at] = (tok[:, at].astype(jnp.float32) + total).astype(jnp.bfloat16)

    each(groups, end_step)


def fused(n, tokens, w_query, w_keyval, w_inner, w_outer, w_attn_out, key_cache, value_cache, lengths):
    rows, width = tokens.shape
    cols, inner, kvw = w_query.shape[1], w_inner.shape[1], w_keyval.shape[1]
    cq, ci = width // cols, width // inner
    half = rows // 2
    all_rows, hrows = n * rows, n * half
    groups = 4 if cq % 4 == 0 else 1
    heads = n * cols // HEAD
    bf, f32 = jnp.bfloat16, jnp.float32
    V, dma = pltpu.VMEM, pltpu.SemaphoreType.DMA
    vmem = pl.BlockSpec(memory_space=pltpu.VMEM)
    hbm = pl.BlockSpec(memory_space=pl.ANY)
    return pl.pallas_call(
        functools.partial(block_kernel, n),
        out_shape=jax.ShapeDtypeStruct(tokens.shape, bf),
        in_specs=[vmem] + [hbm] * 7 + [pl.BlockSpec(memory_space=pltpu.SMEM)],
        out_specs=vmem,
        scratch_shapes=[
            V((cq, cols, cols), bf),
            V((ci, inner, inner), bf),
            V((cq, cols, cols), bf),
            V((kvw, width), bf),
            V(key_cache.shape, bf),
            V(value_cache.shape, bf),
            V((all_rows, width), f32),
            V((all_rows, width), bf),
            V((n, rows, width), bf),
            V((2, n // 2, rows, width), bf),
            V((n // 2, rows, width), bf),
            V((n // 2, rows, width), bf),
            V((n // 2, rows, width), bf),
            V((2 * rows, 128), f32),
            V((2 * rows, 128), f32),
            V((all_rows, cols + 128), f32),
            V((hrows, cols + 128), f32),
            V((n, half, cols + 128), f32),
            V((n, half, cols + 128), f32),
            V((half, heads, HEAD), f32),
            V((all_rows, inner), f32),
            V((all_rows, inner), f32),
            V((all_rows, inner), bf),
            V((n, half, cols), f32),
            V((n, half, cols), f32),
            V((hrows, cols), f32),
            V((hrows, cols), f32),
            dma((cq,)),
            dma((ci,)),
            dma((ci,)),
            dma((cq,)),
            dma((3,)),
            dma((4,)),
            dma((4,)),
            dma((3, n - 1)),
            dma((3, n - 1)),
            dma((groups, n // 2)),
            dma((groups, n // 2)),
        ],
        compiler_params=pltpu.CompilerParams(
            collective_id=0, has_side_effects=True, vmem_limit_bytes=62 * 1024 * 1024
        ),
    )(tokens, w_query, w_keyval.T, w_inner, w_outer, w_attn_out, key_cache, value_cache, lengths)


def plan(n):
    def run(tokens, w_query, w_keyval, w_inner, *rest):
        width, cols, inner = tokens.shape[1], w_query.shape[1], w_inner.shape[1]
        fits = (
            cols % HEAD == 0 and inner % 128 == 0 and width % cols == 0 and width % inner == 0
            and 128 % w_keyval.shape[1] == 0 and tokens.shape[0] == 4 and n * 2 % 16 == 0
        )
        args = (tokens, w_query, w_keyval, w_inner) + rest
        return fused(n, *args) if fits else body(*args)

    return run


def solution(mesh):
    in_specs = (
        P(("groups", "gx"), "yz"),
        P("yz", "gx"),
        P("yz", "gx"),
        P("yz", "gx"),
        P("gx", "yz"),
        P("gx", "yz"),
        P(("groups", "gx", "yz"), None, None),
        P(("groups", "gx", "yz"), None, None),
        P(("groups", "gx", "yz")),
    )
    out_specs = P(("groups", "gx"), "yz")
    return jax.shard_map(plan(mesh.shape["gx"]), mesh=mesh, in_specs=in_specs, out_specs=out_specs, check_vma=False)
```

```python
import functools

import jax
import jax.numpy as jnp
from jax import lax
from jax.experimental import pallas as pl
from jax.experimental.pallas import tpu as pltpu
from jax.sharding import PartitionSpec as P

D = 18432
HEAD = 256


def attend_block(query, key_cache, value_cache, lengths, new_key, new_value):
    scale = 1.0 / HEAD**0.5
    scores = (
        jnp.einsum("rhd,rsd->rhs", query, key_cache, preferred_element_type=jnp.float32) * scale
    )
    positions = lax.broadcasted_iota(jnp.int32, (1, 1, key_cache.shape[1]), 2)
    valid = positions < lengths[:, None, None]
    self_score = (
        jnp.einsum("rhd,rd->rh", query, new_key, preferred_element_type=jnp.float32) * scale
    )
    masked = jnp.where(valid, scores, -jnp.inf)
    top = jnp.maximum(jnp.max(masked, axis=2), self_score)
    cached = jnp.where(valid, jnp.exp(masked - top[:, :, None]), 0.0)
    own = jnp.exp(self_score - top)
    total = jnp.sum(cached, axis=2) + own
    cached_w = (cached / total[:, :, None]).astype(jnp.bfloat16)
    own_w = (own / total).astype(jnp.bfloat16)
    result = jnp.einsum("rhs,rsd->rhd", cached_w, value_cache, preferred_element_type=jnp.float32)
    result = (
        result + own_w.astype(jnp.float32)[:, :, None] * new_value.astype(jnp.float32)[:, None, :]
    )
    return result.astype(jnp.bfloat16).reshape(query.shape[0], query.shape[1] * query.shape[2])


def body(tokens, w_query, w_keyval, w_inner, w_outer, w_attn_out, key_cache, value_cache, lengths):
    x = tokens.astype(jnp.float32)
    moment_one, moment_two = lax.psum((jnp.sum(x, axis=1), jnp.sum(x * x, axis=1)), "yz")
    mean = moment_one / D
    var = moment_two / D - mean * mean
    normed_local = ((x - mean[:, None]) * lax.rsqrt(var + 1e-05)[:, None]).astype(jnp.bfloat16)
    n = lax.axis_size("gx")
    copies = jnp.broadcast_to(normed_local[None], (n,) + normed_local.shape)
    normed = lax.all_to_all(copies, "gx", split_axis=0, concat_axis=0, tiled=True).reshape(
        n * normed_local.shape[0], normed_local.shape[1]
    )
    query_part = jnp.dot(normed, w_query, preferred_element_type=jnp.float32)
    keyval_part = jnp.dot(normed, w_keyval, preferred_element_type=jnp.float32)
    query_rows, keyval_rows = (
        lax.all_to_all(query_part, "gx", split_axis=0, concat_axis=1, tiled=True),
        lax.all_to_all(keyval_part, "gx", split_axis=0, concat_axis=1, tiled=True),
    )
    query_sum, keyval_sum = (
        lax.psum_scatter(query_rows, "yz", scatter_dimension=0, tiled=True),
        lax.psum_scatter(keyval_rows, "yz", scatter_dimension=0, tiled=True),
    )
    inner_part = jnp.dot(normed, w_inner, preferred_element_type=jnp.float32)
    inner_total = inner_part + lax.ppermute(inner_part, "yz", [(0, 1), (1, 0)])
    hidden = jax.nn.gelu(inner_total, approximate=True).astype(jnp.bfloat16)
    local_rows = query_sum.shape[0]
    query = query_sum.astype(jnp.bfloat16).reshape(local_rows, query_sum.shape[1] // HEAD, HEAD)
    keyval = keyval_sum.astype(jnp.bfloat16)
    attended = attend_block(
        query, key_cache, value_cache, lengths, keyval[:, :HEAD], keyval[:, HEAD:]
    )
    paired_rows = lax.all_gather(attended, "yz", axis=0, tiled=True)
    attended_cols = lax.all_to_all(paired_rows, "gx", split_axis=1, concat_axis=0, tiled=True)
    part = jnp.dot(attended_cols, w_attn_out, preferred_element_type=jnp.float32) + jnp.dot(
        hidden, w_outer, preferred_element_type=jnp.float32
    )
    pieces = part.astype(jnp.bfloat16).reshape(n, x.shape[0], x.shape[1])
    pieces = lax.all_to_all(pieces, "gx", split_axis=0, concat_axis=0, tiled=True)
    branch = jnp.sum(pieces.astype(jnp.float32), axis=0)
    return (x + branch).astype(jnp.bfloat16)


def gelu(x):
    c = 0.7978845608028654
    return 0.5 * x * (1.0 + jnp.tanh(c * (x + 0.044715 * (x * x * x))))


def block_kernel(
    n, tok, wq, wkv, wi, wo, wa, kc, vc, lens, out,
    buf_q, buf_i, buf_a, buf_kv, kbuf, vbuf, xf, xb, nbuf, bsend, xrecv, zsend, zrecv, own_sum,
    mom, mom_in, acc_q, half_in, qsend, qrecv, qs, acc_i, inner_in, hb,
    asend, arecv, ahalf, ahalf_in,
    sem_q, sem_i, sem_o, sem_a, sem_l, pair_send, pair_recv, gx_send, gx_recv, g_send, g_recv, b_send, b_recv,
):
    g = lax.axis_index("gx")
    y = lax.axis_index("yz")
    zs = n // 2
    zi, side = lax.div(g, 2), lax.rem(g, 2)
    beside = zi * 2 + 1 - side
    rows, width = tok.shape
    half = rows // 2
    hrows = n * half
    cq, cols = buf_q.shape[0], buf_q.shape[2]
    ci, inner = buf_i.shape[0], buf_i.shape[2]
    per = cols // HEAD
    groups = b_send.shape[0]
    wide = width // groups

    def load_q(i):
        return pltpu.make_async_copy(wq.at[pl.ds(i * cols, cols), :], buf_q.at[i], sem_q.at[i])

    def load_i(i):
        return pltpu.make_async_copy(wi.at[pl.ds(i * inner, inner), :], buf_i.at[i], sem_i.at[i])

    def load_o(i):
        return pltpu.make_async_copy(wo.at[:, pl.ds(i * inner, inner)], buf_i.at[i], sem_o.at[i])

    def load_a(i):
        return pltpu.make_async_copy(wa.at[:, pl.ds(i * cols, cols)], buf_a.at[i], sem_a.at[i])

    load_kv = pltpu.make_async_copy(wkv, buf_kv, sem_l.at[0])
    load_k = pltpu.make_async_copy(kc, kbuf, sem_l.at[1])
    load_v = pltpu.make_async_copy(vc, vbuf, sem_l.at[2])

    def each(count, do):
        def step(i, c):
            do(i)
            return c

        lax.fori_loop(0, count, step, 0)

    each(cq, lambda i: load_q(i).start())
    load_kv.start()
    each(ci, lambda i: load_i(i).start())
    load_k.start()
    load_v.start()
    each(cq, lambda i: load_a(i).start())

    barrier = pltpu.get_barrier_semaphore()
    for i in range(1, n):
        pl.semaphore_signal(
            barrier, inc=1, device_id={"gx": lax.rem(g + i, n)}, device_id_type=pl.DeviceIdType.MESH
        )
    pl.semaphore_signal(barrier, inc=1, device_id={"yz": 1 - y}, device_id_type=pl.DeviceIdType.MESH)

    def to_pair(src, dst, k):
        return pltpu.make_async_remote_copy(
            src_ref=src, dst_ref=dst, send_sem=pair_send.at[k], recv_sem=pair_recv.at[k],
            device_id={"yz": 1 - y}, device_id_type=pl.DeviceIdType.MESH,
        )

    def to_gx(src, dst, send, recv, i):
        return pltpu.make_async_remote_copy(
            src_ref=src, dst_ref=dst, send_sem=send, recv_sem=recv,
            device_id={"gx": lax.rem(g + i, n)}, device_id_type=pl.DeviceIdType.MESH,
        )

    def to_row(src, dst, send, recv, peer):
        return pltpu.make_async_remote_copy(
            src_ref=src, dst_ref=dst, send_sem=send, recv_sem=recv,
            device_id={"gx": peer}, device_id_type=pl.DeviceIdType.MESH,
        )

    x = tok[...].astype(jnp.float32)
    mom[0:rows, :] = jnp.broadcast_to(jnp.sum(x, axis=1, keepdims=True), (rows, 128))
    mom[rows : 2 * rows, :] = jnp.broadcast_to(jnp.sum(x * x, axis=1, keepdims=True), (rows, 128))
    pl.semaphore_wait(barrier, n)
    exchange = to_pair(mom, mom_in, 0)
    exchange.start()
    exchange.wait()
    both = mom[...] + mom_in[...]
    mean = both[0:rows, 0:1] / D
    var = both[rows : 2 * rows, 0:1] / D - mean * mean
    nbuf[g] = ((x - mean) * lax.rsqrt(var + 1e-05)).astype(jnp.bfloat16)

    def g_copy(k, slot, m, peer):
        part = nbuf.at[slot, :, k * wide : (k + 1) * wide]
        return to_row(part, part, g_send.at[k, m], g_recv.at[k, m], peer)

    across = [g_copy(k, g, 0, beside) for k in range(groups)]
    along, onward = [], []
    for k in range(groups):
        along += [g_copy(k, g, i, lax.rem(zi + i, zs) * 2 + side) for i in range(1, zs)]
        onward += [
            g_copy(k, lax.rem(zi + zs - i, zs) * 2 + side, zs - 1 + i, beside) for i in range(1, zs)
        ]
    for k in range(groups):
        for c in along[k * (zs - 1) : (k + 1) * (zs - 1)]:
            c.start()
        across[k].start()
    for c, d in zip(along, onward):
        c.wait_recv()
        d.start()
    for c in across:
        c.wait()
    for c, d in zip(along, onward):
        c.wait_send()
        d.wait()
    for s in range(n):
        v = nbuf[s].astype(jnp.float32)
        xf[s * half : (s + 1) * half, :] = v[0:half, :]
        xf[hrows + s * half : hrows + (s + 1) * half, :] = v[half:rows, :]
    xb[...] = xf[...].astype(jnp.bfloat16)

    acc_q[...] = jnp.zeros_like(acc_q)

    def q_step(i):
        load_q(i).wait()
        acc_q[:, 0:cols] += jnp.dot(
            xb[:, pl.ds(pl.multiple_of(i * cols, 128), cols)], buf_q[i],
            preferred_element_type=jnp.float32,
        )

    each(cq, q_step)
    load_kv.wait()
    kv = lax.dot_general(
        xb[...], buf_kv[...], (((1,), (1,)), ((), ())), preferred_element_type=jnp.float32
    )
    kvw = kv.shape[1]
    spread = 128 // kvw
    kv = jnp.concatenate([kv] * spread, axis=1)
    lane = lax.broadcasted_iota(jnp.int32, kv.shape, 1) // kvw
    acc_q[:, cols : cols + 128] = jnp.where(lane == lax.rem(g, spread), kv, 0.0)

    exchange = to_pair(acc_q.at[pl.ds(pl.multiple_of((1 - y) * hrows, 16), hrows), :], half_in, 1)
    exchange.start()
    exchange.wait()
    mine = acc_q[pl.ds(pl.multiple_of(y * hrows, 16), hrows), :] + half_in[...]
    mine = mine.astype(jnp.bfloat16).astype(jnp.float32)
    for s in range(n):
        qsend[s] = mine[s * half : (s + 1) * half, :]
    q_copies = [
        to_gx(qsend.at[lax.rem(g + i, n)], qrecv.at[g], gx_send.at[1, i - 1], gx_recv.at[1, i - 1], i)
        for i in range(1, n)
    ]
    for c in q_copies:
        c.start()
    qrecv[g] = qsend[g]

    acc_i[...] = jnp.zeros_like(acc_i)

    def i_step(i):
        load_i(i).wait()
        acc_i[...] += jnp.dot(
            xb[:, pl.ds(pl.multiple_of(i * inner, 128), inner)], buf_i[i],
            preferred_element_type=jnp.float32,
        )
        load_o(i).start()

    each(ci, i_step)
    inner_copy = to_pair(acc_i, inner_in, 2)
    inner_copy.start()

    for c in q_copies:
        c.wait()
    load_k.wait()
    load_v.wait()
    scale = 1.0 / HEAD**0.5
    for j in range(half):
        for s in range(n):
            for h in range(per):
                qs[j, s * per + h : s * per + h + 1, :] = qrecv[s, j : j + 1, h * HEAD : (h + 1) * HEAD]
        tails = [qrecv[s, j : j + 1, cols : cols + 128] for s in range(n)]
        lanes = [sum(tails[t * spread + 1 : (t + 1) * spread], tails[t * spread]) for t in range(n // spread)]
        new = jnp.concatenate(lanes, axis=1)
        new_key, new_value = new[:, :HEAD], new[:, HEAD:]
        q = qs[j]
        scores = lax.dot_general(
            q.astype(jnp.bfloat16), kbuf[j], (((1,), (1,)), ((), ())),
            preferred_element_type=jnp.float32,
        ) * scale
        valid = lax.broadcasted_iota(jnp.int32, scores.shape, 1) < lens[j]
        self_score = jnp.sum(q * new_key, axis=1, keepdims=True) * scale
        masked = jnp.where(valid, scores, -jnp.inf)
        top = jnp.maximum(jnp.max(masked, axis=1, keepdims=True), self_score)
        cached = jnp.where(valid, jnp.exp(masked - top), 0.0)
        own = jnp.exp(self_score - top)
        total = jnp.sum(cached, axis=1, keepdims=True) + own
        weights = (cached / total).astype(jnp.bfloat16)
        own_w = (own / total).astype(jnp.bfloat16).astype(jnp.float32)
        res = jnp.dot(weights, vbuf[j], preferred_element_type=jnp.float32) + own_w * new_value
        res = res.astype(jnp.bfloat16).astype(jnp.float32)
        for s in range(n):
            for h in range(per):
                asend[s, j : j + 1, h * HEAD : (h + 1) * HEAD] = res[s * per + h : s * per + h + 1, :]
    a_copies = [
        to_gx(asend.at[lax.rem(g + i, n)], arecv.at[g], gx_send.at[2, i - 1], gx_recv.at[2, i - 1], i)
        for i in range(1, n)
    ]
    for c in a_copies:
        c.start()
    arecv[g] = asend[g]

    inner_copy.wait()
    hb[...] = gelu(acc_i[...] + inner_in[...]).astype(jnp.bfloat16)

    def o_step(i):
        load_o(i).wait()
        xf[:, pl.ds(pl.multiple_of(i * inner, 128), inner)] = jnp.dot(
            hb[...], buf_i[i], preferred_element_type=jnp.float32
        )

    first = ci // 2

    def o_second(i):
        o_step(i + first)

    each(first, o_step)
    for c in a_copies:
        c.wait()
    for s in range(n):
        ahalf[s * half : (s + 1) * half, :] = arecv[s]
    exchange = to_pair(ahalf, ahalf_in, 3)
    exchange.start()
    each(ci - first, o_second)
    exchange.wait()
    a_own, a_other = ahalf[...], ahalf_in[...]
    low = jnp.where(y == 0, a_own, a_other)
    high = jnp.where(y == 0, a_other, a_own)
    att = jnp.concatenate([low, high], axis=0).astype(jnp.bfloat16)
    acc_q[:, 0:cols] = att.astype(jnp.float32)

    def span(k):
        return pl.ds(k * wide if isinstance(k, int) else pl.multiple_of(k * wide, 128), wide)

    def x_copy(k):
        return to_row(
            bsend.at[1 - side, :, :, span(k)], xrecv.at[:, :, span(k)],
            b_send.at[k, 0], b_recv.at[k, 0], beside,
        )

    def z_copy(k, i):
        z = lax.rem(zi + i, zs)
        return to_row(
            zsend.at[z, :, span(k)], zrecv.at[zi, :, span(k)],
            b_send.at[k, i], b_recv.at[k, i], z * 2 + side,
        )

    def sum_x(k):
        x_copy(k).wait()
        for z in range(zs):
            v = own_sum[z, :, span(k)] + xrecv[z, :, span(k)].astype(jnp.float32)
            own_sum[z, :, span(k)] = v
            zsend[z, :, span(k)] = v.astype(jnp.bfloat16)
        for i in range(1, zs):
            z_copy(k, i).start()

    chunks = wide // cols

    def b_step(k):
        a = acc_q[:, 0:cols].astype(jnp.bfloat16)
        for t in range(chunks):
            m = k * chunks + t
            load_a(m).wait()
            at = pl.ds(m * cols if isinstance(m, int) else pl.multiple_of(m * cols, 128), cols)
            r = xf[:, at] + jnp.dot(a, buf_a[m], preferred_element_type=jnp.float32)
            pieces = []
            for s in range(n):
                piece = jnp.concatenate(
                    [r[s * half : (s + 1) * half, :], r[hrows + s * half : hrows + (s + 1) * half, :]],
                    axis=0,
                )
                bsend[s % 2, s // 2, :, at] = piece.astype(jnp.bfloat16)
                pieces.append(piece)
            for z in range(zs):
                own_sum[z, :, at] = jnp.where(side == 0, pieces[2 * z], pieces[2 * z + 1])
        x_copy(k).start()

    def b_next(k):
        b_step(k + 1)
        sum_x(k)

    b_step(0)
    each(groups - 1, b_next)
    sum_x(groups - 1)
    zrecv[zi] = jnp.zeros_like(zrecv[zi])

    def end_step(k):
        for i in range(1, zs):
            z_copy(k, i).wait()
        at = span(k)
        total = own_sum[zi, :, at]
        for z in range(zs):
            total += zrecv[z, :, at].astype(jnp.float32)
        out[:, at] = (tok[:, at].astype(jnp.float32) + total).astype(jnp.bfloat16)

    each(groups, end_step)


def fused(n, tokens, w_query, w_keyval, w_inner, w_outer, w_attn_out, key_cache, value_cache, lengths):
    rows, width = tokens.shape
    cols, inner, kvw = w_query.shape[1], w_inner.shape[1], w_keyval.shape[1]
    cq, ci = width // cols, width // inner
    half = rows // 2
    all_rows, hrows = n * rows, n * half
    groups = 4 if cq % 4 == 0 else 1
    heads = n * cols // HEAD
    bf, f32 = jnp.bfloat16, jnp.float32
    V, dma = pltpu.VMEM, pltpu.SemaphoreType.DMA
    vmem = pl.BlockSpec(memory_space=pltpu.VMEM)
    hbm = pl.BlockSpec(memory_space=pl.ANY)
    return pl.pallas_call(
        functools.partial(block_kernel, n),
        out_shape=jax.ShapeDtypeStruct(tokens.shape, bf),
        in_specs=[vmem] + [hbm] * 7 + [pl.BlockSpec(memory_space=pltpu.SMEM)],
        out_specs=vmem,
        scratch_shapes=[
            V((cq, cols, cols), bf),
            V((ci, inner, inner), bf),
            V((cq, cols, cols), bf),
            V((kvw, width), bf),
            V(key_cache.shape, bf),
            V(value_cache.shape, bf),
            V((all_rows, width), f32),
            V((all_rows, width), bf),
            V((n, rows, width), bf),
            V((2, n // 2, rows, width), bf),
            V((n // 2, rows, width), bf),
            V((n // 2, rows, width), bf),
            V((n // 2, rows, width), bf),
            V((n // 2, rows, width), f32),
            V((2 * rows, 128), f32),
            V((2 * rows, 128), f32),
            V((all_rows, cols + 128), f32),
            V((hrows, cols + 128), f32),
            V((n, half, cols + 128), f32),
            V((n, half, cols + 128), f32),
            V((half, heads, HEAD), f32),
            V((all_rows, inner), f32),
            V((all_rows, inner), f32),
            V((all_rows, inner), bf),
            V((n, half, cols), f32),
            V((n, half, cols), f32),
            V((hrows, cols), f32),
            V((hrows, cols), f32),
            dma((cq,)),
            dma((ci,)),
            dma((ci,)),
            dma((cq,)),
            dma((3,)),
            dma((4,)),
            dma((4,)),
            dma((3, n - 1)),
            dma((3, n - 1)),
            dma((groups, n - 1)),
            dma((groups, n - 1)),
            dma((groups, n // 2)),
            dma((groups, n // 2)),
        ],
        compiler_params=pltpu.CompilerParams(
            collective_id=0, has_side_effects=True, vmem_limit_bytes=62 * 1024 * 1024
        ),
    )(tokens, w_query, w_keyval.T, w_inner, w_outer, w_attn_out, key_cache, value_cache, lengths)


def plan(n):
    def run(tokens, w_query, w_keyval, w_inner, *rest):
        width, cols, inner = tokens.shape[1], w_query.shape[1], w_inner.shape[1]
        fits = (
            cols % HEAD == 0 and inner % 128 == 0 and width % cols == 0 and width % inner == 0
            and 128 % w_keyval.shape[1] == 0 and tokens.shape[0] == 4 and n * 2 % 16 == 0
        )
        args = (tokens, w_query, w_keyval, w_inner) + rest
        return fused(n, *args) if fits else body(*args)

    return run


def solution(mesh):
    in_specs = (
        P(("groups", "gx"), "yz"),
        P("yz", "gx"),
        P("yz", "gx"),
        P("yz", "gx"),
        P("gx", "yz"),
        P("gx", "yz"),
        P(("groups", "gx", "yz"), None, None),
        P(("groups", "gx", "yz"), None, None),
        P(("groups", "gx", "yz")),
    )
    out_specs = P(("groups", "gx"), "yz")
    return jax.shard_map(plan(mesh.shape["gx"]), mesh=mesh, in_specs=in_specs, out_specs=out_specs, check_vma=False)
```
